512 devices in a mesh: prow: 32 (over y, z_lo, core), pcol: 16 (over z_hi, x).
Axes of the slice: x: 4, y: 4, z: 16 (z_hi: 4, z_lo: 4; z = z_hi * 4 + z_lo), core: 2. Of those that a mesh axis runs over, the one named last changes fastest.
Arguments:
- ancestor_inverse: bfloat16 [16384, 16384], P('prow', 'pcol'), may hold values from -6 to 6
- factor_panel: bfloat16 [16384, 2048], P('prow', 'pcol'), may hold values from -0.046875 to 0.046875
- pattern: int32 [128, 16], replicated, may hold values 0 or 1
- diagonal_term: float32 [2048, 128], P('pcol'), may hold values from -6 to 6
Outputs:
- offdiag_inverse: bfloat16 [16384, 2048], P('prow', 'pcol')
- diag_inverse: float32 [2048, 128], P('pcol')
The draws below stay inside these ranges and needn't reach their ends.
All inputs are finite; a program needn't handle non-finite values.
Results may differ from the reference program's by a relative error of at most 0.0065.
Values may be sent and summed in bfloat16 or wider, within the bound.
No kernel may reach another device: no remote copies, remote signals or barrier semaphores. Data moves between devices by JAX's collectives and lax.ppermute only.
A program may use at most 64 MiB of HBM per device.

```python
import jax
import jax.numpy as jnp
from jax import lax

W = 128
R = 16384
NB = 128
NK = 16
KW = 2048


def set_ends(result, key, low, largest):
    spot = [jax.random.randint(jax.random.fold_in(key, axis), (), 0, length) for axis, length in enumerate(result.shape)]
    widest = result.shape.index(max(result.shape))
    next_to = spot[:widest] + [(spot[widest] + 1) % result.shape[widest]] + spot[widest + 1:]
    return result.at[tuple(spot)].set(low).at[tuple(next_to)].set(largest)


def steps_of(rng, shape, pieces, low, high):
    def one(dim, shards_of):
        draws = jax.random.uniform(jax.random.fold_in(jax.random.fold_in(rng, 6), dim), (shards_of,), jnp.float32, low / len(pieces), high / len(pieces))
        return jnp.repeat(jnp.exp(draws), shape[dim] // shards_of).reshape((-1,) + (1,) * (len(shape) - dim - 1))

    level = one(*pieces[0])
    for cut in pieces[1:]:
        level = level * one(*cut)
    return level


def noise(key, extent, scale, reach, cuts=(), kind=jnp.bfloat16):
    result = jax.random.normal(key, extent, jnp.float32) * scale
    if len(cuts) > 0:
        result = steps_of(key, extent, cuts, -0.22, 0.18) * result
    return jnp.clip(result, min=-reach, max=reach).astype(kind)


def setup_inputs(seed: int = 0) -> dict:
    streams_of = jax.random.split(jax.random.key(seed), 5)
    return {
        "ancestor_inverse": noise(streams_of[0], (R, R), 1.0, 6.0, ((0, 32), (1, 16))),
        "factor_panel": noise(streams_of[1], (R, KW), R ** -0.5, 0.046875, ((0, 32), (1, 16))),
        "pattern": set_ends((jax.random.randint(streams_of[2], (NB, NK), 0, 3) < 1).astype(jnp.int32), jax.random.fold_in(streams_of[2], 1), 0, 1),
        "diagonal_term": noise(streams_of[3], (KW, W), 1.0, 6.0, ((0, 16),), jnp.float32),
    }


def reference(ancestor_inverse, factor_panel, pattern, diagonal_term):
    expanded = jnp.repeat(jnp.repeat(pattern, W, axis=0), W, axis=1)
    masked = factor_panel * expanded.astype(jnp.bfloat16)
    product = jnp.dot(ancestor_inverse.astype(jnp.float32), masked.astype(jnp.float32), precision=lax.Precision.HIGHEST)
    offdiag_inverse = (-product * expanded.astype(jnp.float32)).astype(jnp.bfloat16)
    left = masked.astype(jnp.float32).reshape(R, NK, W)
    right = product.reshape(R, NK, W)
    blocks = jnp.einsum("rka,rkb->kab", left, right, precision=lax.Precision.HIGHEST)
    diag_inverse = diagonal_term + blocks.reshape(KW, W)
    return offdiag_inverse, diag_inverse
```

```python
import jax
import jax.numpy as jnp
from jax import lax
from jax.sharding import PartitionSpec as P

W = 128
BF = jnp.bfloat16
F32 = jnp.float32
PROW, PCOL = 32, 16


def groups(count, key):
    found = {}
    for i in range(count):
        found.setdefault(key(i), []).append(i)
    return list(found.values())


ZLO = groups(PROW, lambda r: (r // 8, r % 2))
Y = groups(PROW, lambda r: r % 8)
X = groups(PCOL, lambda c: c // 4)
ZHI = groups(PCOL, lambda c: c % 4)
SWAP = [(r, r ^ 1) for r in range(PROW)]


def target(r, c):
    z_hi, x = c // 4, c % 4
    core = z_hi // 2
    z_lo = 2 * (z_hi % 2) + r % 2
    return ((x * 4 + z_lo) * 2 + core) * PCOL + r // 2


SPREAD = [(r * PCOL + c, target(r, c)) for r in range(PROW) for c in range(PCOL)]


def gather(block, axis, members):
    count = len(members[0])
    copies = jnp.broadcast_to(block[None], (count,) + block.shape)
    return lax.all_to_all(copies, axis, 0, 0, axis_index_groups=members)


def on_device(ancestor_inverse, factor_panel, pattern, diagonal_term):
    row_index = lax.axis_index("prow")
    col_index = lax.axis_index("pcol")
    core = row_index % 2
    rows = factor_panel.shape[0]
    row_blocks = rows // W
    local_mask = lax.dynamic_slice(
        pattern, (row_index * row_blocks, col_index), (row_blocks, 1)
    )
    expanded = jnp.broadcast_to(local_mask[:, :, None], (row_blocks, W, W)).reshape(rows, W)
    masked = factor_panel * expanded.astype(BF)
    other_inverse = lax.ppermute(ancestor_inverse, "prow", SWAP)
    block = lax.ppermute(masked, ("prow", "pcol"), SPREAD)
    panel = gather(gather(block, "prow", ZLO), "prow", Y)
    panel = panel.reshape(8, 2 * rows, W)

    def times(inverse):
        out = jnp.einsum("rc,kcn->krn", inverse, panel, preferred_element_type=F32)
        return out.astype(BF).reshape(4, 2, 1, rows, W)

    partial = jnp.concatenate([times(ancestor_inverse), times(other_inverse)], axis=2)
    partial = lax.all_to_all(partial, "pcol", 0, 0, axis_index_groups=X)
    partial = jnp.sum(partial.astype(F32), axis=0).astype(BF)
    mine = partial[:, 0]
    theirs = lax.ppermute(partial[:, 1], "prow", SWAP)
    low = jnp.where(core == 0, mine, theirs)
    high = jnp.where(core == 0, theirs, mine)
    partial = jnp.concatenate([low, high], axis=0)
    partial = lax.all_to_all(partial, "pcol", 0, 0, axis_index_groups=ZHI)
    product = jnp.sum(partial.astype(F32), axis=0)
    offdiag = (-product * expanded.astype(F32)).astype(BF)
    sums = lax.dot_general(
        masked, product.astype(BF), (((0,), (0,)), ((), ())), preferred_element_type=F32
    )
    pieces = sums.astype(BF).reshape(PROW, W // PROW, W)
    pieces = lax.all_to_all(pieces, "prow", 0, 0)
    piece = jnp.sum(pieces.astype(F32), axis=0).astype(BF)
    copies = jnp.broadcast_to(piece[None], (PROW,) + piece.shape)
    blocks = lax.all_to_all(copies, "prow", 0, 0).reshape(W, W)
    return offdiag, diagonal_term + blocks.astype(F32)


def solution(mesh):
    in_specs = (P("prow", "pcol"), P("prow", "pcol"), P(), P("pcol", None))
    out_specs = (P("prow", "pcol"), P("pcol", None))
    return jax.shard_map(
        on_device, mesh=mesh, in_specs=in_specs, out_specs=out_specs, check_vma=False
    )
```

```python
import jax
import jax.numpy as jnp
from jax import lax
from jax.experimental import pallas as pl
from jax.experimental.pallas import tpu as pltpu
from jax.sharding import PartitionSpec as P

W = 128
BF = jnp.bfloat16
F32 = jnp.float32
PROW, PCOL = 32, 16
BOTH = ("prow", "pcol")
TAIL = 1
COST = 18
VMEM_MB = 32


def groups(count, key):
    found = {}
    for i in range(count):
        found.setdefault(key(i), []).append(i)
    return list(found.values())


ZLO = groups(PROW, lambda r: (r // 8, r % 2))
Y = groups(PROW, lambda r: r % 8)
YC = groups(PROW, lambda r: r // 2 % 4)
ZC = groups(PROW, lambda r: r // 8)
X = groups(PCOL, lambda c: c // 4)
ZHI = groups(PCOL, lambda c: c % 4)


def place(y, z_lo, core, z_hi, x):
    return ((y * 4 + z_lo) * 2 + core) * PCOL + z_hi * 4 + x


def moves(to):
    pairs = []
    for device in range(PROW * PCOL):
        r, c = divmod(device, PCOL)
        pairs.append((device, place(*to(r // 8, r // 2 % 4, r % 2, c // 4, c % 4))))
    return pairs


def send(block, to):
    return lax.ppermute(block, BOTH, moves(to))


def spread(y, z_lo, core, z_hi, x):
    return z_lo, 2 * (z_hi % 2) + core, z_hi // 2, y, x


def swap(y, z_lo, core, z_hi, x):
    return y, z_lo, 1 - core, z_hi, x


def along_y(d):
    return lambda y, z_lo, core, z_hi, x: ((y + d) % 4, z_lo, core, z_hi, x)


def along_z_lo(d):
    return lambda y, z_lo, core, z_hi, x: (y, (z_lo + d) % 4, core, z_hi, x)


def along_x(d):
    return lambda y, z_lo, core, z_hi, x: (y, z_lo, core, z_hi, (x + d) % 4)


def home(s, t):
    return lambda y, z_lo, core, z_hi, x: (y, z_lo, (z_hi // 2) ^ s, 2 * core + ((z_hi % 2) ^ t), x)


def pick(stack, index):
    return lax.dynamic_index_in_dim(stack, index, 0, keepdims=False)


def gather(block, axis, members):
    count = len(members[0])
    copies = jnp.broadcast_to(block[None], (count,) + block.shape)
    return lax.all_to_all(copies, axis, 0, 0, axis_index_groups=members)


def times_kernel(swapped, panel, mine, other, first, second):
    tile = 256

    def product(part, rows):
        total = jnp.dot(part[0, rows], panel[0], preferred_element_type=F32)
        for d in range(1, 4):
            total += jnp.dot(part[d, rows], panel[d], preferred_element_type=F32)
        return total.astype(BF)

    for start in range(0, mine.shape[1], tile):
        rows = pl.ds(start, tile)
        ours = product(mine, rows)
        others = product(other, rows)

        @pl.when(swapped[0] == 0)
        def _():
            first[rows] = ours
            second[rows] = others

        @pl.when(swapped[0] != 0)
        def _():
            first[rows] = others
            second[rows] = ours


def times(swapped, mine, other, panel):
    count, rows, depth = mine.shape
    return pl.pallas_call(
        times_kernel,
        in_specs=[pl.BlockSpec(memory_space=pltpu.SMEM)] + [pl.BlockSpec(memory_space=pltpu.VMEM)] * 3,
        out_specs=[pl.BlockSpec(memory_space=pltpu.VMEM)] * 2,
        out_shape=[jax.ShapeDtypeStruct((rows, W), BF)] * 2,
        compiler_params=pltpu.CompilerParams(vmem_limit_bytes=VMEM_MB * 1024 * 1024),
        cost_estimate=pl.CostEstimate(
            flops=2 * 2 * count * rows * depth * W, bytes_accessed=COST * rows * depth, transcendentals=0
        ),
    )(swapped, panel, mine, other)


def on_device(ancestor_inverse, factor_panel, pattern, diagonal_term):
    row_index = lax.axis_index("prow")
    col_index = lax.axis_index("pcol")
    y, z_lo, core = row_index // 8, row_index // 2 % 4, row_index % 2
    z_hi, x = col_index // 4, col_index % 4
    rows = factor_panel.shape[0]
    row_blocks = rows // W
    local_mask = lax.dynamic_slice(
        pattern, (row_index * row_blocks, col_index), (row_blocks, 1)
    )
    expanded = jnp.broadcast_to(local_mask[:, :, None], (row_blocks, W, W)).reshape(rows, W)
    masked = factor_panel * expanded.astype(BF)
    mine = gather(ancestor_inverse, "pcol", X)
    block = send(masked, spread)
    near = jnp.stack([block] + [send(block, along_z_lo(d)) for d in range(1, 4)])
    near, mine = lax.optimization_barrier((near, mine))
    other = send(mine, swap)
    far = []
    for t in range(2):
        b = (z_hi % 2) ^ t
        both = jnp.stack([pick(near, (z_lo - 2 * b - j) % 4) for j in range(2)])
        far.append(gather(both, "prow", Y).reshape(4, 2 * rows, W))
    swapped = ((z_hi // 2) ^ core)[None]
    product = 0
    for t in range(2):
        pieces = times(swapped, mine, other, far[t])
        for s in range(2):
            product += send(pieces[s], home(s, t)).astype(F32)
    offdiag = (-product * expanded.astype(F32)).astype(BF)
    sums = lax.dot_general(
        masked, product.astype(BF), (((0,), (0,)), ((), ())), preferred_element_type=F32
    )
    if TAIL == 0:
        pieces = sums.astype(BF).reshape(PROW, W // PROW, W)
        pieces = lax.all_to_all(pieces, "prow", 0, 0)
        piece = jnp.sum(pieces.astype(F32), axis=0).astype(BF)
        blocks = gather(piece, "prow", [list(range(PROW))]).reshape(W, W).astype(F32)
    else:
        wide, narrow = ((YC, ZLO), (ZC, Y))[TAIL - 1]
        blocks = jnp.sum(gather(sums.astype(BF), "prow", wide).astype(F32), axis=0)
        blocks = jnp.sum(gather(blocks.astype(BF), "prow", narrow).astype(F32), axis=0)
    return offdiag, diagonal_term + blocks


def solution(mesh):
    in_specs = (P("prow", "pcol"), P("prow", "pcol"), P(), P("pcol", None))
    out_specs = (P("prow", "pcol"), P("pcol", None))
    return jax.shard_map(
        on_device, mesh=mesh, in_specs=in_specs, out_specs=out_specs, check_vma=False
    )
```

```python
import jax
import jax.numpy as jnp
from jax import lax
from jax.experimental import pallas as pl
from jax.experimental.pallas import tpu as pltpu
from jax.sharding import PartitionSpec as P

W = 128
BF = jnp.bfloat16
F32 = jnp.float32
PROW, PCOL = 32, 16
BOTH = ("prow", "pcol")


def groups(count, key):
    found = {}
    for i in range(count):
        found.setdefault(key(i), []).append(i)
    return list(found.values())


ZLO = groups(PROW, lambda r: (r // 8, r % 2))
Y = groups(PROW, lambda r: r % 8)
YC = groups(PROW, lambda r: r // 2 % 4)


def place(y, z_lo, core, z_hi, x):
    return ((y * 4 + z_lo) * 2 + core) * PCOL + z_hi * 4 + x


def moves(to):
    pairs = []
    for device in range(PROW * PCOL):
        r, c = divmod(device, PCOL)
        where = to(r // 8, r // 2 % 4, r % 2, c // 4, c % 4)
        if where is not None:
            pairs.append((device, place(*where)))
    return pairs


def send(block, to):
    return lax.ppermute(block, BOTH, moves(to))


def spread_y(y, z_lo, core, z_hi, x):
    return (y + z_lo) % 4, z_lo, core, z_hi, x


def spread_z(y, z_lo, core, z_hi, x):
    return y, 2 * (z_hi % 2) + core, z_hi // 2, (y - z_lo) % 4, x


def swap(y, z_lo, core, z_hi, x):
    return y, z_lo, 1 - core, z_hi, x


def along_x(d):
    return lambda y, z_lo, core, z_hi, x: (y, z_lo, core, z_hi, (x + d) % 4)


def relay(step):
    def to(y, z_lo, core, z_hi, x):
        if core != z_hi // 2:
            return y, z_lo, core, (z_hi + step) % 4, x
        if z_hi % 2 == (step < 0):
            return y, z_lo, 1 - core, z_hi, x
        return None

    return to


def onward(relayed):
    def to(y, z_lo, core, z_hi, x):
        target = 2 * core + 1 - z_hi % 2
        rising = target == (z_hi + 1) % 4
        return y, z_lo, int(rising != relayed), target, x

    return to


def gather(block, axis, members):
    count = len(members[0])
    copies = jnp.broadcast_to(block[None], (count,) + block.shape)
    return lax.all_to_all(copies, axis, 0, 0, axis_index_groups=members)


def times_kernel(order, panel, *refs):
    ours, others, (out, panel_here, parts, total, sems) = refs[:5], refs[5:10], refs[10:]
    rows, half = parts.shape[1], parts.shape[1] // 2
    copies = [[pltpu.make_async_copy(panel, panel_here, sems.at[0])]]
    for d in range(4):
        pairs = []
        for core, blocks in enumerate((ours, others)):
            slot = parts.at[2 * d + core]
            if d < 3:
                pairs.append((blocks[d], slot))
            else:
                pairs += [(blocks[3], slot.at[pl.ds(0, half)]), (blocks[4], slot.at[pl.ds(half, half)])]
        first = sum(len(group) for group in copies)
        copies.append([pltpu.make_async_copy(a, b, sems.at[first + i]) for i, (a, b) in enumerate(pairs)])
    for group in copies:
        for copy in group:
            copy.start()
    for copy in copies[0]:
        copy.wait()
    for d in range(4):
        for copy in copies[d + 1]:
            copy.wait()
        columns = jnp.concatenate([panel_here[order[d], 0], panel_here[order[d], 1]], axis=1)
        for core in range(2):
            here = pl.ds(core * rows, rows)
            term = jnp.dot(parts[2 * d + core], columns, preferred_element_type=F32)
            total[here] = term if d == 0 else total[here] + term
    for core in range(2):
        for b in range(2):
            slot = jnp.where(order[4] == b, order[5], order[6])
            out[slot ^ core] = total[pl.ds(core * rows, rows), pl.ds(b * W, W)].astype(BF)


def times(order, ours, others, panel):
    rows, depth = ours[0].shape
    return pl.pallas_call(
        times_kernel,
        in_specs=[pl.BlockSpec(memory_space=pltpu.SMEM)] + [pl.BlockSpec(memory_space=pl.ANY)] * 11,
        out_specs=pl.BlockSpec(memory_space=pltpu.VMEM),
        out_shape=jax.ShapeDtypeStruct((4, rows, W), BF),
        scratch_shapes=[
            pltpu.VMEM(panel.shape, BF),
            pltpu.VMEM((8, rows, depth), BF),
            pltpu.VMEM((2 * rows, 2 * W), F32),
            pltpu.SemaphoreType.DMA((11,)),
        ],
        compiler_params=pltpu.CompilerParams(vmem_limit_bytes=56 * 1024 * 1024),
        cost_estimate=pl.CostEstimate(
            flops=32 * rows * depth * W, bytes_accessed=18 * rows * depth, transcendentals=0
        ),
    )(order, panel, *ours, *others)


def on_device(ancestor_inverse, factor_panel, pattern, diagonal_term):
    row_index = lax.axis_index("prow")
    col_index = lax.axis_index("pcol")
    y, z_lo, core = row_index // 8, row_index // 2 % 4, row_index % 2
    z_hi, x = col_index // 4, col_index % 4
    rows = factor_panel.shape[0]
    row_blocks = rows // W
    local_mask = lax.dynamic_slice(
        pattern, (row_index * row_blocks, col_index), (row_blocks, 1)
    )
    expanded = jnp.broadcast_to(local_mask[:, :, None], (row_blocks, W, W)).reshape(rows, W)
    masked = factor_panel * expanded.astype(BF)
    ancestor_inverse, masked = lax.optimization_barrier((ancestor_inverse, masked))
    half = rows // 2
    before = send(ancestor_inverse, along_x(1))
    after = send(ancestor_inverse, along_x(3))
    block = send(send(masked, spread_y), spread_z)
    block, before, after = lax.optimization_barrier((block, before, after))
    near = gather(block, "prow", ZLO)
    swapped = [send(part, swap) for part in (ancestor_inverse, before, after)]
    near, *swapped = lax.optimization_barrier((near, *swapped))
    panel = gather(near, "prow", Y).reshape(4, 2, 2 * rows, W)
    top = send(before[:half], along_x(1))
    bottom = send(after[half:], along_x(3))
    ours = [ancestor_inverse, before, after, top, bottom]
    others = swapped + [send(part, swap) for part in ours[3:]]
    stays = core == z_hi // 2
    rising = 2 * core + 1 - z_hi % 2 == (z_hi + 1) % 4
    order = jnp.stack(
        [(x - d + z_hi) % 4 for d in (0, 1, 3, 2)]
        + [z_hi % 2, jnp.where(stays, 1 - z_hi % 2, core), jnp.where(rising == (core == 0), 3, 2)]
    )
    up, down, direct, last = times(order, ours, others, panel)
    from_below, from_above = send(up, relay(1)), send(down, relay(-1))
    product = send(direct, onward(False)).astype(F32)
    kept = jnp.where(stays, jnp.where(z_hi % 2 == 0, down, up), jnp.where(rising, from_above, from_below))
    relayed = jnp.where(rising, from_below, from_above)
    last = (last.astype(F32) + relayed.astype(F32)).astype(BF)
    product += kept.astype(F32) + send(last, onward(True)).astype(F32)
    offdiag = (-product * expanded.astype(F32)).astype(BF)
    sums = lax.dot_general(
        masked, product.astype(BF), (((0,), (0,)), ((), ())), preferred_element_type=F32
    )
    for members in (YC, ZLO):
        sums = jnp.sum(gather(sums.astype(BF), "prow", members).astype(F32), axis=0)
    return offdiag, diagonal_term + sums


def solution(mesh):
    in_specs = (P("prow", "pcol"), P("prow", "pcol"), P(), P("pcol", None))
    out_specs = (P("prow", "pcol"), P("pcol", None))
    return jax.shard_map(
        on_device, mesh=mesh, in_specs=in_specs, out_specs=out_specs, check_vma=False
    )
```

```python
import jax
import jax.numpy as jnp
from jax import lax
from jax.experimental import pallas as pl
from jax.experimental.pallas import tpu as pltpu
from jax.sharding import PartitionSpec as P

W = 128
BF = jnp.bfloat16
F32 = jnp.float32
PROW, PCOL = 32, 16
BOTH = ("prow", "pcol")


def groups(count, key):
    found = {}
    for i in range(count):
        found.setdefault(key(i), []).append(i)
    return list(found.values())


ZLO = groups(PROW, lambda r: (r // 8, r % 2))
Y = groups(PROW, lambda r: r % 8)
YC = groups(PROW, lambda r: r // 2 % 4)


def place(y, z_lo, core, z_hi, x):
    return ((y * 4 + z_lo) * 2 + core) * PCOL + z_hi * 4 + x


def moves(to):
    pairs = []
    for device in range(PROW * PCOL):
        r, c = divmod(device, PCOL)
        where = to(r // 8, r // 2 % 4, r % 2, c // 4, c % 4)
        if where is not None:
            pairs.append((device, place(*where)))
    return pairs


def send(block, to):
    return lax.ppermute(block, BOTH, moves(to))


def spread_y(y, z_lo, core, z_hi, x):
    return (y + z_lo) % 4, z_lo, core, z_hi, x


def spread_z(y, z_lo, core, z_hi, x):
    return y, 2 * (z_hi % 2) + core, z_hi // 2, (y - z_lo) % 4, x


def swap(y, z_lo, core, z_hi, x):
    return y, z_lo, 1 - core, z_hi, x


def along_x(d):
    return lambda y, z_lo, core, z_hi, x: (y, z_lo, core, z_hi, (x + d) % 4)


def relay(step):
    def to(y, z_lo, core, z_hi, x):
        if core != z_hi // 2:
            return y, z_lo, core, (z_hi + step) % 4, x
        if z_hi % 2 == (step < 0):
            return y, z_lo, 1 - core, z_hi, x
        return None

    return to


def onward(relayed):
    def to(y, z_lo, core, z_hi, x):
        target = 2 * core + 1 - z_hi % 2
        rising = target == (z_hi + 1) % 4
        return y, z_lo, int(rising != relayed), target, x

    return to


def gather(block, axis, members):
    count = len(members[0])
    copies = jnp.broadcast_to(block[None], (count,) + block.shape)
    return lax.all_to_all(copies, axis, 0, 0, axis_index_groups=members)


def times_kernel(order, panel, *refs):
    ours, others, (out, panel_here, parts, total, sems) = refs[:5], refs[5:10], refs[10:]
    rows, half = parts.shape[1], parts.shape[1] // 2
    copies = [[pltpu.make_async_copy(panel, panel_here, sems.at[0])]]
    for d in range(4):
        pairs = []
        for core, blocks in enumerate((ours, others)):
            slot = parts.at[2 * d + core]
            if d < 3:
                pairs.append((blocks[d], slot))
            else:
                pairs += [(blocks[3], slot.at[pl.ds(0, half)]), (blocks[4], slot.at[pl.ds(half, half)])]
        first = sum(len(group) for group in copies)
        copies.append([pltpu.make_async_copy(a, b, sems.at[first + i]) for i, (a, b) in enumerate(pairs)])
    for group in copies:
        for copy in group:
            copy.start()
    for copy in copies[0]:
        copy.wait()
    for d in range(4):
        for copy in copies[d + 1]:
            copy.wait()
        columns = jnp.concatenate([panel_here[order[d], 0], panel_here[order[d], 1]], axis=1)
        for core in range(2):
            here = pl.ds(core * rows, rows)
            term = jnp.dot(parts[2 * d + core], columns, preferred_element_type=F32)
            total[here] = term if d == 0 else total[here] + term
    for core in range(2):
        for b in range(2):
            slot = jnp.where(order[4] == b, order[5], order[6])
            out[slot ^ core] = total[pl.ds(core * rows, rows), pl.ds(b * W, W)].astype(BF)


def times(order, ours, others, panel):
    rows, depth = ours[0].shape
    return pl.pallas_call(
        times_kernel,
        in_specs=[pl.BlockSpec(memory_space=pltpu.SMEM)] + [pl.BlockSpec(memory_space=pl.ANY)] * 11,
        out_specs=pl.BlockSpec(memory_space=pltpu.VMEM),
        out_shape=jax.ShapeDtypeStruct((4, rows, W), BF),
        scratch_shapes=[
            pltpu.VMEM(panel.shape, BF),
            pltpu.VMEM((8, rows, depth), BF),
            pltpu.VMEM((2 * rows, 2 * W), F32),
            pltpu.SemaphoreType.DMA((11,)),
        ],
        compiler_params=pltpu.CompilerParams(vmem_limit_bytes=56 * 1024 * 1024),
        cost_estimate=pl.CostEstimate(
            flops=32 * rows * depth * W, bytes_accessed=18 * rows * depth, transcendentals=0
        ),
    )(order, panel, *ours, *others)


def on_device(ancestor_inverse, factor_panel, pattern, diagonal_term):
    row_index = lax.axis_index("prow")
    col_index = lax.axis_index("pcol")
    y, z_lo, core = row_index // 8, row_index // 2 % 4, row_index % 2
    z_hi, x = col_index // 4, col_index % 4
    rows = factor_panel.shape[0]
    row_blocks = rows // W
    local_mask = lax.dynamic_slice(
        pattern, (row_index * row_blocks, col_index), (row_blocks, 1)
    )
    expanded = jnp.broadcast_to(local_mask[:, :, None], (row_blocks, W, W)).reshape(rows, W)
    masked = factor_panel * expanded.astype(BF)
    half = rows // 2
    before = send(ancestor_inverse, along_x(1))
    after = send(ancestor_inverse, along_x(3))
    block = send(send(masked, spread_y), spread_z)
    block, before, after = lax.optimization_barrier((block, before, after))
    near = gather(block, "prow", ZLO)
    swapped = [send(part, swap) for part in (ancestor_inverse, before, after)]
    top, bottom = before[:half], after[half:]
    near, top, bottom, *swapped = lax.optimization_barrier((near, top, bottom, *swapped))
    panel = gather(near, "prow", Y).reshape(4, 2, 2 * rows, W)
    top = send(top, along_x(1))
    bottom = send(bottom, along_x(3))
    ours = [ancestor_inverse, before, after, top, bottom]
    others = swapped + [send(part, swap) for part in ours[3:]]
    stays = core == z_hi // 2
    rising = 2 * core + 1 - z_hi % 2 == (z_hi + 1) % 4
    order = jnp.stack(
        [(x - d + z_hi) % 4 for d in (0, 1, 3, 2)]
        + [z_hi % 2, jnp.where(stays, 1 - z_hi % 2, core), jnp.where(rising == (core == 0), 3, 2)]
    )
    up, down, direct, last = times(order, ours, others, panel)
    from_below, from_above = send(up, relay(1)), send(down, relay(-1))
    product = send(direct, onward(False)).astype(F32)
    kept = jnp.where(stays, jnp.where(z_hi % 2 == 0, down, up), jnp.where(rising, from_above, from_below))
    relayed = jnp.where(rising, from_below, from_above)
    last = (last.astype(F32) + relayed.astype(F32)).astype(BF)
    product += kept.astype(F32) + send(last, onward(True)).astype(F32)
    offdiag = (-product * expanded.astype(F32)).astype(BF)
    sums = lax.dot_general(
        masked, product.astype(BF), (((0,), (0,)), ((), ())), preferred_element_type=F32
    )
    for members in (YC, ZLO):
        sums = jnp.sum(gather(sums.astype(BF), "prow", members).astype(F32), axis=0)
    return offdiag, diagonal_term + sums


def solution(mesh):
    in_specs = (P("prow", "pcol"), P("prow", "pcol"), P(), P("pcol", None))
    out_specs = (P("prow", "pcol"), P("pcol", None))
    return jax.shard_map(
        on_device, mesh=mesh, in_specs=in_specs, out_specs=out_specs, check_vma=False
    )
```

```python
import jax
import jax.numpy as jnp
from jax import lax
from jax.experimental import pallas as pl
from jax.experimental.pallas import tpu as pltpu
from jax.sharding import PartitionSpec as P

W = 128
BF = jnp.bfloat16
F32 = jnp.float32
PROW, PCOL = 32, 16
BOTH = ("prow", "pcol")


def groups(count, key):
    found = {}
    for i in range(count):
        found.setdefault(key(i), []).append(i)
    return list(found.values())


ZLO = groups(PROW, lambda r: (r // 8, r % 2))
Y = groups(PROW, lambda r: r % 8)
YC = groups(PROW, lambda r: r // 2 % 4)


def place(y, z_lo, core, z_hi, x):
    return ((y * 4 + z_lo) * 2 + core) * PCOL + z_hi * 4 + x


def moves(to):
    pairs = []
    for device in range(PROW * PCOL):
        r, c = divmod(device, PCOL)
        where = to(r // 8, r // 2 % 4, r % 2, c // 4, c % 4)
        if where is not None:
            pairs.append((device, place(*where)))
    return pairs


def send(block, to):
    return lax.ppermute(block, BOTH, moves(to))


def spread_y(y, z_lo, core, z_hi, x):
    return (y + z_lo) % 4, z_lo, core, z_hi, x


def spread_z(y, z_lo, core, z_hi, x):
    return y, 2 * (z_hi % 2) + core, z_hi // 2, (y - z_lo) % 4, x


def swap(y, z_lo, core, z_hi, x):
    return y, z_lo, 1 - core, z_hi, x


def along_x(d):
    return lambda y, z_lo, core, z_hi, x: (y, z_lo, core, z_hi, (x + d) % 4)


def relay(step):
    def to(y, z_lo, core, z_hi, x):
        if core != z_hi // 2:
            return y, z_lo, core, (z_hi + step) % 4, x
        if z_hi % 2 == (step < 0):
            return y, z_lo, 1 - core, z_hi, x
        return None

    return to


def onward(relayed):
    def to(y, z_lo, core, z_hi, x):
        target = 2 * core + 1 - z_hi % 2
        rising = target == (z_hi + 1) % 4
        return y, z_lo, int(rising != relayed), target, x

    return to


def gather(block, axis, members):
    count = len(members[0])
    copies = jnp.broadcast_to(block[None], (count,) + block.shape)
    return lax.all_to_all(copies, axis, 0, 0, axis_index_groups=members)


def times_kernel(order, panel, *refs):
    ours, others, (out, panel_here, parts, total, sems) = refs[:5], refs[5:10], refs[10:]
    rows, half = parts.shape[1], parts.shape[1] // 2
    copies = [[pltpu.make_async_copy(panel, panel_here, sems.at[0])]]
    for d in range(4):
        pairs = []
        for core, blocks in enumerate((ours, others)):
            slot = parts.at[2 * d + core]
            if d < 3:
                pairs.append((blocks[d], slot))
            else:
                pairs += [(blocks[3], slot.at[pl.ds(0, half)]), (blocks[4], slot.at[pl.ds(half, half)])]
        first = sum(len(group) for group in copies)
        copies.append([pltpu.make_async_copy(a, b, sems.at[first + i]) for i, (a, b) in enumerate(pairs)])
    for group in copies:
        for copy in group:
            copy.start()
    for copy in copies[0]:
        copy.wait()
    for d in range(4):
        for copy in copies[d + 1]:
            copy.wait()
        columns = jnp.concatenate([panel_here[order[d], 0], panel_here[order[d], 1]], axis=1)
        for core in range(2):
            here = pl.ds(core * rows, rows)
            term = jnp.dot(parts[2 * d + core], columns, preferred_element_type=F32)
            total[here] = term if d == 0 else total[here] + term
    for core in range(2):
        for b in range(2):
            slot = jnp.where(order[4] == b, order[5], order[6])
            out[slot ^ core] = total[pl.ds(core * rows, rows), pl.ds(b * W, W)].astype(BF)


def times(order, ours, others, panel):
    rows, depth = ours[0].shape
    return pl.pallas_call(
        times_kernel,
        in_specs=[pl.BlockSpec(memory_space=pltpu.SMEM)] + [pl.BlockSpec(memory_space=pl.ANY)] * 11,
        out_specs=pl.BlockSpec(memory_space=pltpu.VMEM),
        out_shape=jax.ShapeDtypeStruct((4, rows, W), BF),
        scratch_shapes=[
            pltpu.VMEM(panel.shape, BF),
            pltpu.VMEM((8, rows, depth), BF),
            pltpu.VMEM((2 * rows, 2 * W), F32),
            pltpu.SemaphoreType.DMA((11,)),
        ],
        compiler_params=pltpu.CompilerParams(vmem_limit_bytes=56 * 1024 * 1024),
        cost_estimate=pl.CostEstimate(
            flops=32 * rows * depth * W, bytes_accessed=18 * rows * depth, transcendentals=0
        ),
    )(order, panel, *ours, *others)


def on_device(ancestor_inverse, factor_panel, pattern, diagonal_term):
    row_index = lax.axis_index("prow")
    col_index = lax.axis_index("pcol")
    y, z_lo, core = row_index // 8, row_index // 2 % 4, row_index % 2
    z_hi, x = col_index // 4, col_index % 4
    rows = factor_panel.shape[0]
    row_blocks = rows // W

    def mask_of(r, c):
        mask = lax.dynamic_slice(pattern, (r * row_blocks, c), (row_blocks, 1))
        return jnp.broadcast_to(mask[:, :, None], (row_blocks, W, W)).reshape(rows, W)

    expanded = mask_of(row_index, col_index)
    masked = factor_panel * expanded.astype(BF)
    half = rows // 2
    before = send(ancestor_inverse, along_x(1))
    after = send(ancestor_inverse, along_x(3))
    block = send(send(factor_panel, spread_y), spread_z)
    block, before, after = lax.optimization_barrier((block, before, after))
    came_row = z_hi * 8 + (y - z_hi) % 4 * 2 + z_lo % 2
    came_col = (2 * core + z_lo // 2) * 4 + x
    block = block * mask_of(came_row, came_col).astype(BF)
    near = gather(block, "prow", ZLO)
    swapped = [send(part, swap) for part in (ancestor_inverse, before, after)]
    top, bottom = before[:half], after[half:]
    near, top, bottom, *swapped = lax.optimization_barrier((near, top, bottom, *swapped))
    panel = gather(near, "prow", Y).reshape(4, 2, 2 * rows, W)
    top = send(top, along_x(1))
    bottom = send(bottom, along_x(3))
    ours = [ancestor_inverse, before, after, top, bottom]
    others = swapped + [send(part, swap) for part in ours[3:]]
    stays = core == z_hi // 2
    rising = 2 * core + 1 - z_hi % 2 == (z_hi + 1) % 4
    order = jnp.stack(
        [(x - d + z_hi) % 4 for d in (0, 1, 3, 2)]
        + [z_hi % 2, jnp.where(stays, 1 - z_hi % 2, core), jnp.where(rising == (core == 0), 3, 2)]
    )
    up, down, direct, last = times(order, ours, others, panel)
    from_below, from_above = send(up, relay(1)), send(down, relay(-1))
    product = send(direct, onward(False)).astype(F32)
    kept = jnp.where(stays, jnp.where(z_hi % 2 == 0, down, up), jnp.where(rising, from_above, from_below))
    relayed = jnp.where(rising, from_below, from_above)
    last = (last.astype(F32) + relayed.astype(F32)).astype(BF)
    product += kept.astype(F32) + send(last, onward(True)).astype(F32)
    offdiag = (-product * expanded.astype(F32)).astype(BF)
    sums = lax.dot_general(
        masked, product.astype(BF), (((0,), (0,)), ((), ())), preferred_element_type=F32
    )
    for members in (YC, ZLO):
        sums = jnp.sum(gather(sums.astype(BF), "prow", members).astype(F32), axis=0)
    return offdiag, diagonal_term + sums


def solution(mesh):
    in_specs = (P("prow", "pcol"), P("prow", "pcol"), P(), P("pcol", None))
    out_specs = (P("prow", "pcol"), P("pcol", None))
    return jax.shard_map(
        on_device, mesh=mesh, in_specs=in_specs, out_specs=out_specs, check_vma=False
    )
```
